256 devices in a mesh: worker: 8 (over y, z_hi), fsdp: 32 (over z_lo, x, core).
Axes of the slice: x: 4, y: 4, z: 8 (z_hi: 2, z_lo: 4; z = z_hi * 4 + z_lo), core: 2. Of those that a mesh axis runs over, the one named last changes fastest.
Arguments:
- activations: bfloat16 [131072, 4608], P(('worker', 'fsdp')), may hold values from -6 to 6
- key_target: bfloat16 [131072, 1024], P(('worker', 'fsdp')), may hold values from -6 to 6
- key_weight: bfloat16 [36864, 1024], P(('worker', 'fsdp')), may hold values from -0.09375 to 0.09375
- fragment_base: float32 [512, 4608], P('fsdp'), may hold values from -6 to 6
- fragment_momentum: float32 [512, 4608], P('fsdp'), may hold values from -6 to 6
- delta_codes: int32 [4096, 4608], P(('worker', 'fsdp')), may hold values from 0 to 15
- block_scale: float32 [4096, 36], P(('worker', 'fsdp')), may hold values from 0.5 to 5
- code_table: float32 [16], replicated, may hold values from -1 to 1
Outputs:
- weight_grad: float32 [36864, 1024], P(('worker', 'fsdp'))
- input_grad: bfloat16 [131072, 4608], P(('worker', 'fsdp'))
- new_base: float32 [512, 4608], P('fsdp')
- new_momentum: float32 [512, 4608], P('fsdp')
The draws below stay inside these ranges and needn't reach their ends.
All inputs are finite; a program needn't handle non-finite values.
Results may differ from the reference program's by a relative error of at most 0.0047.
Values may be sent and summed in bfloat16 or wider, within the bound.
A program may use at most 128 MiB of HBM per device.

```python
import math
import jax
import jax.numpy as jnp
from jax import lax

D = 4608
KV = 1024
BLOCK = 128
CODES = 16
GROUP_TOKENS = 16384
TOKENS = 131072
FRAG = 512
N_WORKER = 8


def plant(array, own_key, low, largest):
    place = [jax.random.randint(jax.random.fold_in(own_key, axis), (), 0, length) for axis, length in enumerate(array.shape)]
    main_axis = array.shape.index(max(array.shape))
    neighbour = place[:main_axis] + [(place[main_axis] + 1) % array.shape[main_axis]] + place[main_axis + 1:]
    return array.at[tuple(place)].set(low).at[tuple(neighbour)].set(largest)


def level_of(own_key, shape, split, smallest, largest):
    def one(position, shards_of):
        draws = jax.random.uniform(jax.random.fold_in(jax.random.fold_in(own_key, 6), position), (shards_of,), jnp.float32, smallest / len(split), largest / len(split))
        return jnp.repeat(jnp.exp(draws), shape[position] // shards_of).reshape((-1,) + (1,) * (len(shape) - position - 1))

    gain = one(*split[0])
    for cut in split[1:]:
        gain = gain * one(*cut)
    return gain


def centred(own_key, extent, width, most, split=(), dtype=jnp.bfloat16):
    drawn = jax.random.normal(own_key, extent, jnp.float32) * width
    if len(split) > 0:
        drawn = level_of(own_key, extent, split, -0.22, 0.18) * drawn
    return jnp.clip(drawn, min=-most, max=most).astype(dtype)


def setup_inputs(seed: int = 0) -> dict:
    keys = jax.random.split(jax.random.key(seed), 9)
    return {
        "activations": centred(keys[0], (TOKENS, D), 1.0, 6.0, ((0, 256),)),
        "key_target": centred(keys[1], (TOKENS, KV), 1.0, 6.0, ((0, 256),)),
        "key_weight": centred(keys[2], (N_WORKER * D, KV), D ** -0.5, 0.09375, ((0, 256),)),
        "fragment_base": centred(keys[3], (FRAG, D), 1.0, 6.0, ((0, 32),), jnp.float32),
        "fragment_momentum": centred(keys[4], (FRAG, D), 1.0, 6.0, ((0, 32),), jnp.float32),
        "delta_codes": plant(jax.random.randint(keys[5], (N_WORKER * FRAG, D), 0, CODES), jax.random.fold_in(keys[5], 1), 0, CODES - 1).astype(jnp.int32),
        "block_scale": jnp.clip(jnp.exp(math.log(5.0) - 2.3025851 * jax.random.uniform(keys[6], (N_WORKER * FRAG, D // BLOCK), jnp.float32) ** level_of(keys[6], (N_WORKER * FRAG, D // BLOCK), ((0, 256),), -0.2, 0.2)), 0.5, 5.0),
        "code_table": jnp.clip(jax.random.uniform(keys[7], (CODES,), jnp.float32, -1.0, 1.0), -1.0, 1.0),
    }


outer_rate = 0.7
outer_momentum = 0.9

def one_group(pieces):
    group_acts, group_target, group_weight = pieces
    projected = jnp.dot(group_acts, group_weight, preferred_element_type=jnp.float32)
    errors = (projected - group_target.astype(jnp.float32)).astype(jnp.bfloat16)
    input_grad = jnp.dot(errors, group_weight.T, preferred_element_type=jnp.float32).astype(jnp.bfloat16)
    group_sum = jnp.dot(group_acts.T, errors, preferred_element_type=jnp.float32)
    weight_grad = group_sum / jnp.sqrt(jnp.float32(GROUP_TOKENS))
    return (weight_grad, input_grad)

def reference(activations, key_target, key_weight, fragment_base, fragment_momentum, delta_codes, block_scale, code_table):
    stacked = (activations.reshape(N_WORKER, GROUP_TOKENS, D), key_target.reshape(N_WORKER, GROUP_TOKENS, KV), key_weight.reshape(N_WORKER, D, KV))
    weight_grad, input_grad = lax.map(one_group, stacked)
    weight_grad = weight_grad.reshape(N_WORKER * D, KV)
    input_grad = input_grad.reshape(TOKENS, D)
    values = code_table[delta_codes]
    rows_all = values.shape[0]
    delta = (values.reshape(rows_all, D // BLOCK, BLOCK) * block_scale[:, :, None]).reshape(rows_all, D)
    mean_delta = lax.optimization_barrier(jnp.sum(delta.reshape(N_WORKER, FRAG, D), axis=0)) / N_WORKER
    new_momentum = outer_momentum * fragment_momentum + mean_delta
    new_base = fragment_base - outer_rate * (mean_delta + outer_momentum * new_momentum)
    return (weight_grad, input_grad, new_base, new_momentum)
```

```python
import functools

import jax
import jax.numpy as jnp
from jax import lax
from jax.experimental import pallas as pl
from jax.experimental.pallas import tpu as pltpu
from jax.sharding import PartitionSpec as P

BLOCK = 128
NZ, NX, NC = 4, 4, 2
PARTS = 4

MESH = pl.DeviceIdType.MESH
F32, BF16 = jnp.float32, jnp.bfloat16

outer_rate = 0.7
outer_momentum = 0.9


def outer_update(mean_delta, base_rows, momentum_rows):
    momentum_next = outer_momentum * momentum_rows + mean_delta
    base_next = base_rows - outer_rate * (mean_delta + outer_momentum * momentum_next)
    return (base_next, momentum_next)


def kernel(
    a_hbm, t_hbm, w_hbm, wg_hbm, ig_hbm,
    a, at, t, w, e, g, dr, x2r, x1r, zr, wg, ig,
    lsem, wsem, tsem, osem,
    ag_s, ag_r, rs_s, rs_r,
):
    tokens, d = a.shape
    rows, cw = w.shape[4], w.shape[5]
    scale = 1.0 / (tokens * NZ * NX * NC) ** 0.5
    wk = lax.axis_index("worker")
    f = lax.axis_index("fsdp")
    z, x, c = f // (NX * NC), lax.rem(f // NC, NX), lax.rem(f, NC)
    xp, xm, xo, co = lax.rem(x + 1, NX), lax.rem(x + 3, NX), lax.rem(x + 2, NX), 1 - c

    def dev(zz, xx, cc):
        return (wk, (zz * NX + xx) * NC + cc)

    zup = [lax.rem(z + k, NZ) for k in range(NZ)]
    zdn = [lax.rem(z + NZ - k, NZ) for k in range(NZ)]
    DP, DM, DS = dev(z, xp, c), dev(z, xm, c), dev(z, x, co)

    for s in range(PARTS):
        cols = pl.ds(s * cw, cw)
        pltpu.make_async_copy(w_hbm.at[:, cols], w.at[s, z, x, c], wsem.at[s]).start()
    pltpu.make_async_copy(a_hbm, a, lsem).start()
    for s in range(PARTS):
        pltpu.make_async_copy(t_hbm.at[:, pl.ds(s * cw, cw)], t.at[s], tsem.at[s]).start()

    barrier = pltpu.get_barrier_semaphore()
    partners = [dev(zup[k], x, c) for k in (1, 2, 3)] + [DP, DM, DS]
    for p in partners:
        pl.semaphore_signal(barrier, inc=1, device_id=p, device_id_type=MESH)
    pl.semaphore_wait(barrier, len(partners))

    sent = []

    def send(src, dst, ss, rs, to):
        cp = pltpu.make_async_remote_copy(
            src_ref=src, dst_ref=dst, send_sem=ss, recv_sem=rs, device_id=to, device_id_type=MESH
        )
        cp.start()
        sent.append(cp)

    def arrive(dst, rs):
        pltpu.make_async_remote_copy(
            src_ref=dst, dst_ref=dst, send_sem=rs, recv_sem=rs, device_id=DS, device_id_type=MESH
        ).wait_recv()

    def z_send(s):
        pltpu.make_async_copy(w_hbm.at[:, pl.ds(s * cw, cw)], w.at[s, z, x, c], wsem.at[s]).wait()
        for k in (3, 2, 1):
            blk = w.at[s, z, x, c]
            send(blk, blk, ag_s.at[s, k], ag_r.at[s, k], dev(zup[k], x, c))

    def z_wait(s):
        for k in (1, 2, 3):
            arrive(w.at[s, zdn[k], x, c], ag_r.at[s, k])

    def x1_send(s):
        line = w.at[s, :, x, c]
        send(line, line, ag_s.at[s, 4], ag_r.at[s, 4], DP)
        send(line, line, ag_s.at[s, 5], ag_r.at[s, 5], DM)

    def x2_send(s):
        arrive(w.at[s, :, xm, c], ag_r.at[s, 4])
        up = w.at[s, pl.ds(0, 2), xm, c]
        send(up, up, ag_s.at[s, 6], ag_r.at[s, 6], DP)
        arrive(w.at[s, :, xp, c], ag_r.at[s, 5])
        down = w.at[s, pl.ds(2, 2), xp, c]
        send(down, down, ag_s.at[s, 7], ag_r.at[s, 7], DM)

    def x2_wait(s):
        arrive(w.at[s, pl.ds(0, 2), xo, c], ag_r.at[s, 6])
        arrive(w.at[s, pl.ds(2, 2), xo, c], ag_r.at[s, 7])

    def d_send(s, k):
        line = w.at[s, :, (x, xp, xm, xo)[k], c]
        send(line, line, ag_s.at[s, 8 + k], ag_r.at[s, 8 + k], DS)

    def d_wait(s):
        for k in range(4):
            arrive(w.at[s, :, (x, xp, xm, xo)[k], co], ag_r.at[s, 8 + k])

    def transpose():
        pltpu.make_async_copy(a_hbm, a, lsem).wait()
        slab = d // NZ
        for j in range(NZ):
            at[j] = a[:, j * slab : (j + 1) * slab].T.reshape(NX, NC * rows, tokens)

    mt = min(256, tokens)

    def project(s):
        pltpu.make_async_copy(t_hbm.at[:, pl.ds(s * cw, cw)], t.at[s], tsem.at[s]).wait()

        @pl.loop(0, tokens // mt)
        def _(m):
            r = pl.ds(pl.multiple_of(m * mt, mt), mt)
            p = jnp.dot(a[r, :], w[s].reshape(d, cw), preferred_element_type=F32)
            e[s, r, :] = (p - t[s, r, :].astype(F32)).astype(BF16)

    def grad_rows(s, k):
        xt = (xo, xp, xm, x)[k]

        @pl.loop(0, NZ)
        def _(j):
            q = jnp.dot(at[j, xt], e[s], preferred_element_type=F32)
            g[s, j, xt] = q.astype(BF16).reshape(NC, rows, cw)

        send(g.at[s, :, xt, co], dr.at[s, :, xt], rs_s.at[s, k], rs_r.at[s, k], DS)

    def back(j):
        slab = d // NZ
        c0 = j * slab

        @pl.loop(0, tokens // mt)
        def _(m):
            r = pl.ds(pl.multiple_of(m * mt, mt), mt)
            acc = None
            for s in range(PARTS):
                q = lax.dot_general(
                    e[s, r, :], w[s, j].reshape(slab, cw), (((1,), (1,)), ((), ())),
                    preferred_element_type=F32,
                )
                acc = q if acc is None else acc + q
            ig[r, c0 : c0 + slab] = acc.astype(BF16)

        pltpu.make_async_copy(ig.at[:, pl.ds(c0, slab)], ig_hbm.at[:, pl.ds(c0, slab)], osem.at[j]).start()

    def rx2(s):
        arrive(dr.at[s, :, xo], rs_r.at[s, 0])

        @pl.loop(0, NZ)
        def _(j):
            g[s, j, xo, c] = (g[s, j, xo, c].astype(F32) + dr[s, j, xo].astype(F32)).astype(BF16)

        send(g.at[s, pl.ds(0, 2), xo, c], x2r.at[s, 0], rs_s.at[s, 4], rs_r.at[s, 4], DP)
        send(g.at[s, pl.ds(2, 2), xo, c], x2r.at[s, 1], rs_s.at[s, 5], rs_r.at[s, 5], DM)

    def rx1(s):
        arrive(dr.at[s, :, xp], rs_r.at[s, 1])
        arrive(dr.at[s, :, xm], rs_r.at[s, 2])
        arrive(x2r.at[s, 0], rs_r.at[s, 4])
        arrive(x2r.at[s, 1], rs_r.at[s, 5])
        for j in range(NZ):
            up = g[s, j, xp, c].astype(F32) + dr[s, j, xp].astype(F32)
            if j < 2:
                up = up + x2r[s, 0, j].astype(F32)
            g[s, j, xp, c] = up.astype(BF16)
        send(g.at[s, :, xp, c], x1r.at[s, 0], rs_s.at[s, 6], rs_r.at[s, 6], DP)
        for j in range(NZ):
            down = g[s, j, xm, c].astype(F32) + dr[s, j, xm].astype(F32)
            if j >= 2:
                down = down + x2r[s, 1, j - 2].astype(F32)
            g[s, j, xm, c] = down.astype(BF16)
        send(g.at[s, :, xm, c], x1r.at[s, 1], rs_s.at[s, 7], rs_r.at[s, 7], DM)

    def x_sum(s, j):
        return (
            g[s, j, x, c].astype(F32)
            + dr[s, j, x].astype(F32)
            + x1r[s, 0, j].astype(F32)
            + x1r[s, 1, j].astype(F32)
        )

    def rz(s):
        arrive(dr.at[s, :, x], rs_r.at[s, 3])
        arrive(x1r.at[s, 0], rs_r.at[s, 6])
        arrive(x1r.at[s, 1], rs_r.at[s, 7])
        for k in (3, 2, 1):
            j = zup[k]
            g[s, j, x, c] = x_sum(s, j).astype(BF16)
            send(g.at[s, j, x, c], zr.at[s, k - 1], rs_s.at[s, 7 + k], rs_r.at[s, 7 + k], dev(j, x, c))
        wg[:, s * cw : (s + 1) * cw] = x_sum(s, z)

    def rf(s):
        for k in (1, 2, 3):
            arrive(zr.at[s, k - 1], rs_r.at[s, 7 + k])
        cols = slice(s * cw, (s + 1) * cw)
        total = wg[:, cols]
        for k in range(3):
            total = total + zr[s, k].astype(F32)
        wg[:, cols] = total * scale
        pltpu.make_async_copy(
            wg.at[:, pl.ds(s * cw, cw)], wg_hbm.at[:, pl.ds(s * cw, cw)], osem.at[NZ + s]
        ).start()

    last = PARTS - 1
    z_send(0)
    transpose()
    z_wait(0)
    x1_send(0)
    z_send(1)
    d_send(0, 0)
    for s in range(PARTS):
        x2_send(s)
        d_send(s, 1)
        d_send(s, 2)
        if s < last:
            z_wait(s + 1)
            x1_send(s + 1)
            d_send(s + 1, 0)
        if s + 1 < last:
            z_send(s + 2)
        x2_wait(s)
        d_send(s, 3)
        if s > 0:
            rx1(s - 1)
        d_wait(s)
        project(s)
        for k in range(4):
            grad_rows(s, k)
        if s > 0:
            rz(s - 1)
        rx2(s)
        if s > 0:
            rf(s - 1)
    back(0)
    rx1(last)
    back(1)
    back(2)
    rz(last)
    back(3)
    rf(last)

    for cp in sent:
        cp.wait_send()
    slab = d // NZ
    for j in range(NZ):
        cols = pl.ds(j * slab, slab)
        pltpu.make_async_copy(ig.at[:, cols], ig_hbm.at[:, cols], osem.at[j]).wait()
    for s in range(PARTS):
        cols = pl.ds(s * cw, cw)
        pltpu.make_async_copy(wg.at[:, cols], wg_hbm.at[:, cols], osem.at[NZ + s]).wait()


def inner_step(activations, key_target, key_weight):
    tokens, d = activations.shape
    rows, kv = key_weight.shape
    cw = kv // PARTS
    blk = (rows, cw)
    dma = pltpu.SemaphoreType.DMA
    return pl.pallas_call(
        kernel,
        out_shape=(
            jax.ShapeDtypeStruct((rows, kv), F32),
            jax.ShapeDtypeStruct((tokens, d), BF16),
        ),
        in_specs=[pl.BlockSpec(memory_space=pl.ANY)] * 3,
        out_specs=[pl.BlockSpec(memory_space=pl.ANY)] * 2,
        scratch_shapes=[
            pltpu.VMEM((tokens, d), BF16),
            pltpu.VMEM((NZ, NX, NC * rows, tokens), BF16),
            pltpu.VMEM((PARTS, tokens, cw), BF16),
            pltpu.VMEM((PARTS, NZ, NX, NC) + blk, BF16),
            pltpu.VMEM((PARTS, tokens, cw), BF16),
            pltpu.VMEM((PARTS, NZ, NX, NC) + blk, BF16),
            pltpu.VMEM((PARTS, NZ, NX) + blk, BF16),
            pltpu.VMEM((PARTS, 2, 2) + blk, BF16),
            pltpu.VMEM((PARTS, 2, NZ) + blk, BF16),
            pltpu.VMEM((PARTS, NZ - 1) + blk, BF16),
            pltpu.VMEM((rows, kv), F32),
            pltpu.VMEM((tokens, d), BF16),
            dma,
            dma((PARTS,)),
            dma((PARTS,)),
            dma((NZ + PARTS,)),
            dma((PARTS, 12)),
            dma((PARTS, 12)),
            dma((PARTS, 11)),
            dma((PARTS, 11)),
        ],
        compiler_params=pltpu.CompilerParams(
            collective_id=0, has_side_effects=True, vmem_limit_bytes=60 * 2**20
        ),
        cost_estimate=pl.CostEstimate(
            flops=6 * tokens * d * kv, bytes_accessed=64 * 2**20, transcendentals=0
        ),
        name="inner_step",
    )(activations, key_target, key_weight)


def body(
    activations,
    key_target,
    key_weight,
    fragment_base,
    fragment_momentum,
    delta_codes,
    block_scale,
    code_table,
):
    levels = jnp.arange(code_table.shape[0], dtype=jnp.int32)
    matches = delta_codes[:, :, None] == levels
    values = jnp.sum(jnp.where(matches, code_table, jnp.float32(0.0)), axis=-1)
    rows_here = delta_codes.shape[0]
    width = delta_codes.shape[1]
    deltas = (values.reshape(rows_here, width // BLOCK, BLOCK) * block_scale[:, :, None]).reshape(
        rows_here, width
    )
    workers = lax.axis_size("worker")
    total_delta = lax.psum(deltas, "worker")
    weight_grad, input_grad = inner_step(activations, key_target, key_weight)
    mean_delta = total_delta / workers
    new_base, new_momentum = outer_update(mean_delta, fragment_base, fragment_momentum)
    return (weight_grad, input_grad, new_base, new_momentum)


def solution(mesh):
    placed = (
        P(("worker", "fsdp"), None),
        P(("worker", "fsdp"), None),
        P(("worker", "fsdp"), None),
        P("fsdp", None),
        P("fsdp", None),
        P(("worker", "fsdp"), None),
        P(("worker", "fsdp"), None),
        P(),
    )
    return jax.shard_map(
        body,
        mesh=mesh,
        in_specs=placed,
        out_specs=(
            P(("worker", "fsdp"), None),
            P(("worker", "fsdp"), None),
            P("fsdp", None),
            P("fsdp", None),
        ),
        check_vma=False,
    )
```

```python
import jax
import jax.numpy as jnp
from jax import lax
from jax.experimental import pallas as pl
from jax.experimental.pallas import tpu as pltpu
from jax.sharding import PartitionSpec as P

BLOCK = 128
NZ, NX, NC = 4, 4, 2
NY, NH = 4, 2
WIDTHS = (1, 2, 2, 2, 1)
MIXED = (0, 1, 1, 1, 0)

MESH = pl.DeviceIdType.MESH
F32, BF16 = jnp.float32, jnp.bfloat16

outer_rate = 0.7
outer_momentum = 0.9


def outer_update(mean_delta, base_rows, momentum_rows):
    momentum_next = outer_momentum * momentum_rows + mean_delta
    base_next = base_rows - outer_rate * (mean_delta + outer_momentum * momentum_next)
    return (base_next, momentum_next)


def kernel(
    table, a_hbm, t_hbm, w_hbm, code_hbm, scale_hbm,
    wg_hbm, ig_hbm, mean_hbm,
    a, at, t, w, e, g, dr, x2r, x1r, zr, zc, hx2, hx1, wg, ig,
    code, bscale, dl, dyr, dz, mean,
    lsem, csem, wsem, tsem, osem, isem, msem,
    ag_s, ag_r, rs_s, rs_r, dl_s, dl_r,
):
    parts = len(w)
    tokens, d = a.shape
    rows = w[0].shape[3]
    width = [p.shape[4] for p in w]
    start = [sum(width[:s]) for s in range(parts)]
    half = rows // 9
    low = [rows - 2 * half * m for m in MIXED]
    lows = [pl.ds(0, n) for n in low]
    first = rows - 2 * half
    hi, hi0, hi1 = pl.ds(first, 2 * half), pl.ds(first, half), pl.ds(first + half, half)
    scale = 1.0 / (tokens * NZ * NX * NC) ** 0.5
    slab = d // NZ
    quarter = d // NY

    wk = lax.axis_index("worker")
    f = lax.axis_index("fsdp")
    y, h = wk // NH, lax.rem(wk, NH)
    z, x, c = f // (NX * NC), lax.rem(f // NC, NX), lax.rem(f, NC)
    xp, xm, xo, co = lax.rem(x + 1, NX), lax.rem(x + 3, NX), lax.rem(x + 2, NX), 1 - c
    lines = (xo, xp, xm, x)

    def dev(zz, xx, cc):
        return (wk, (zz * NX + xx) * NC + cc)

    zup = [lax.rem(z + k, NZ) for k in range(NZ)]
    zdn = [lax.rem(z + NZ - k, NZ) for k in range(NZ)]
    yup = [lax.rem(y + k, NY) for k in range(NY)]
    ydn = [lax.rem(y + NY - k, NY) for k in range(NY)]
    DP, DM, DS = dev(z, xp, c), dev(z, xm, c), dev(z, x, co)
    DU, DD = dev(lax.rem(z + 1, NZ), x, c), dev(lax.rem(z + 3, NZ), x, c)
    DH = (y * NH + 1 - h, f)

    def cols(s):
        return pl.ds(start[s], width[s])

    def w_in(s):
        return pltpu.make_async_copy(w_hbm.at[:, cols(s)], w[s].at[z, x, c], wsem.at[s])

    def t_in(s):
        return pltpu.make_async_copy(t_hbm.at[:, cols(s)], t[s], tsem.at[s])

    a_in = pltpu.make_async_copy(a_hbm, a, lsem)
    code_in = pltpu.make_async_copy(code_hbm, code, csem.at[0])
    scale_in = pltpu.make_async_copy(scale_hbm, bscale, csem.at[1])

    for s in range(parts):
        w_in(s).start()
    code_in.start()
    scale_in.start()
    a_in.start()
    for s in range(parts):
        t_in(s).start()

    barrier = pltpu.get_barrier_semaphore()
    partners = [dev(zup[k], x, c) for k in (1, 2, 3)] + [DP, DM, DS, DH]
    partners += [(yup[k] * NH + h, f) for k in (1, 2, 3)]
    for p in partners:
        pl.semaphore_signal(barrier, inc=1, device_id=p, device_id_type=MESH)
    pl.semaphore_wait(barrier, len(partners))

    sent = []

    def send(src, dst, ss, rs, to, cond=None):
        cp = pltpu.make_async_remote_copy(
            src_ref=src, dst_ref=dst, send_sem=ss, recv_sem=rs, device_id=to, device_id_type=MESH
        )
        if cond is None:
            cp.start()
        else:
            pl.when(cond)(cp.start)
        sent.append((cp, cond))

    def arrive(dst, rs):
        pltpu.make_async_remote_copy(
            src_ref=dst, dst_ref=dst, send_sem=rs, recv_sem=rs, device_id=DS, device_id_type=MESH
        ).wait_recv()

    def guard(ok):
        def wrap(step):
            def run(s, *k):
                if ok(s):
                    step(s, *k)

            return run

        return wrap

    there = guard(lambda s: 0 <= s < parts)
    if_mixed = guard(lambda s: 0 <= s < parts and MIXED[s])

    @there
    def z_send(s):
        w_in(s).wait()
        for k in (3, 2, 1):
            blk = w[s].at[z, x, c, lows[s]]
            send(blk, blk, ag_s.at[s, k - 1], ag_r.at[s, k - 1], dev(zup[k], x, c))

    @there
    def z_wait(s):
        for k in (1, 2, 3):
            arrive(w[s].at[zdn[k], x, c, lows[s]], ag_r.at[s, k - 1])

    @there
    def x1_send(s):
        line = w[s].at[:, x, c, lows[s]]
        send(line, line, ag_s.at[s, 3], ag_r.at[s, 3], DP)
        send(line, line, ag_s.at[s, 4], ag_r.at[s, 4], DM)

    @there
    def x2_send(s):
        arrive(w[s].at[:, xm, c, lows[s]], ag_r.at[s, 3])
        up = w[s].at[pl.ds(0, 2), xm, c, lows[s]]
        send(up, up, ag_s.at[s, 5], ag_r.at[s, 5], DP)
        arrive(w[s].at[:, xp, c, lows[s]], ag_r.at[s, 4])
        down = w[s].at[pl.ds(2, 2), xp, c, lows[s]]
        send(down, down, ag_s.at[s, 6], ag_r.at[s, 6], DM)

    @there
    def x2_wait(s):
        arrive(w[s].at[pl.ds(0, 2), xo, c, lows[s]], ag_r.at[s, 5])
        arrive(w[s].at[pl.ds(2, 2), xo, c, lows[s]], ag_r.at[s, 6])

    @there
    def d_send(s, k):
        line = w[s].at[:, lines[k], c, lows[s]]
        send(line, line, ag_s.at[s, 7 + k], ag_r.at[s, 7 + k], DS)

    @if_mixed
    def d_send_hi(s):
        rest = w[s].at[:, :, c, hi]
        send(rest, rest, ag_s.at[s, 11], ag_r.at[s, 11], DS)

    @there
    def d_wait(s):
        for k in range(4):
            arrive(w[s].at[:, lines[k], co, lows[s]], ag_r.at[s, 7 + k])
        if MIXED[s]:
            arrive(w[s].at[:, :, co, hi], ag_r.at[s, 11])

    @if_mixed
    def h1_send(s):
        blk = w[s].at[z, x, c, hi]
        send(blk, blk, ag_s.at[s, 12], ag_r.at[s, 12], DP)
        send(blk, blk, ag_s.at[s, 13], ag_r.at[s, 13], DM)

    @if_mixed
    def h2_send(s):
        arrive(w[s].at[z, xm, c, hi], ag_r.at[s, 12])
        up = w[s].at[z, xm, c, hi0]
        send(up, up, ag_s.at[s, 14], ag_r.at[s, 14], DP)
        arrive(w[s].at[z, xp, c, hi], ag_r.at[s, 13])
        down = w[s].at[z, xp, c, hi1]
        send(down, down, ag_s.at[s, 15], ag_r.at[s, 15], DM)

    @if_mixed
    def h2_wait(s):
        arrive(w[s].at[z, xo, c, hi0], ag_r.at[s, 14])
        arrive(w[s].at[z, xo, c, hi1], ag_r.at[s, 15])

    @if_mixed
    def hop_send(s, k):
        up, dn = w[s].at[zdn[k - 1], :, c, hi], w[s].at[zup[k - 1], :, c, hi]
        send(up, up, ag_s.at[s, 15 + k], ag_r.at[s, 15 + k], DU, (z >= k - 1) & (z < NZ - 1))
        send(dn, dn, ag_s.at[s, 18 + k], ag_r.at[s, 18 + k], DD, (z + k <= NZ) & (z > 0))

    @if_mixed
    def hop_wait(s, k):
        pl.when(z >= k)(lambda: arrive(w[s].at[zdn[k], :, c, hi], ag_r.at[s, 15 + k]))
        pl.when(z + k < NZ)(lambda: arrive(w[s].at[zup[k], :, c, hi], ag_r.at[s, 18 + k]))

    def transpose():
        a_in.wait()
        for j in range(NZ):
            at[j] = a[:, j * slab : (j + 1) * slab].T.reshape(NX, NC * rows, tokens)

    @there
    def project(s):
        t_in(s).wait()
        p = jnp.dot(a[...], w[s][...].reshape(d, width[s]), preferred_element_type=F32)
        e[s][...] = (p - t[s][...].astype(F32)).astype(BF16)

    @there
    def grad_rows(s, k):
        xt = lines[k]
        q = jnp.dot(at[:, xt].reshape(slab, tokens), e[s][...], preferred_element_type=F32)
        g[s][:, xt] = q.astype(BF16).reshape(NZ, NC, rows, width[s])
        send(g[s].at[:, xt, co], dr[s].at[:, xt], rs_s.at[s, k], rs_r.at[s, k], DS)

    def back(j):
        er = jnp.concatenate([e[s][...] for s in range(parts)], axis=1)
        wr = jnp.concatenate([w[s][j].reshape(slab, width[s]) for s in range(parts)], axis=1)
        q = lax.dot_general(er, wr, (((1,), (1,)), ((), ())), preferred_element_type=F32)
        ig[:, j * slab : (j + 1) * slab] = q.astype(BF16)
        ig_out(j).start()

    def ig_out(j):
        here = pl.ds(j * slab, slab)
        return pltpu.make_async_copy(ig.at[:, here], ig_hbm.at[:, here], isem.at[j])

    def wg_out(s):
        return pltpu.make_async_copy(wg.at[:, cols(s)], wg_hbm.at[:, cols(s)], osem.at[s])

    def plus(u, v):
        return u.astype(F32) + v.astype(F32)

    def merge(s, k):
        xt = lines[k]
        arrive(dr[s].at[:, xt], rs_r.at[s, k])
        g[s][:, xt, c] = plus(g[s][:, xt, c], dr[s][:, xt]).astype(BF16)

    @there
    def r1(s):
        merge(s, 0)
        send(g[s].at[pl.ds(0, 2), xo, c, lows[s]], x2r[s].at[0], rs_s.at[s, 4], rs_r.at[s, 4], DP)
        send(g[s].at[pl.ds(2, 2), xo, c, lows[s]], x2r[s].at[1], rs_s.at[s, 5], rs_r.at[s, 5], DM)
        for k in (1, 2, 3):
            merge(s, k)
        if MIXED[s]:
            hop(s, 1)

    def hop(s, k):
        up, dn = zup[NZ - k], zdn[NZ - k]
        goes_up, goes_dn = z <= k - 1, z >= NZ - k
        if k > 1:

            @pl.when(goes_up & (z > 0))
            def _():
                arrive(zc[s].at[0, k - 2], rs_r.at[s, 9 + k])
                g[s][up, :, c, first:] = plus(g[s][up, :, c, first:], zc[s][0, k - 2]).astype(BF16)

            @pl.when(goes_dn & (z < NZ - 1))
            def _():
                arrive(zc[s].at[1, k - 2], rs_r.at[s, 12 + k])
                g[s][dn, :, c, first:] = plus(g[s][dn, :, c, first:], zc[s][1, k - 2]).astype(BF16)

        send(g[s].at[up, :, c, hi], zc[s].at[0, k - 1], rs_s.at[s, 10 + k], rs_r.at[s, 10 + k], DU, goes_up)
        send(g[s].at[dn, :, c, hi], zc[s].at[1, k - 1], rs_s.at[s, 13 + k], rs_r.at[s, 13 + k], DD, goes_dn)

    @there
    def r2(s):
        arrive(x2r[s].at[0], rs_r.at[s, 4])
        g[s][0:2, xp, c, :low[s]] = plus(g[s][0:2, xp, c, :low[s]], x2r[s][0]).astype(BF16)
        send(g[s].at[:, xp, c, lows[s]], x1r[s].at[0], rs_s.at[s, 6], rs_r.at[s, 6], DP)
        arrive(x2r[s].at[1], rs_r.at[s, 5])
        g[s][2:4, xm, c, :low[s]] = plus(g[s][2:4, xm, c, :low[s]], x2r[s][1]).astype(BF16)
        send(g[s].at[:, xm, c, lows[s]], x1r[s].at[1], rs_s.at[s, 7], rs_r.at[s, 7], DM)
        if MIXED[s]:
            hop(s, 2)

    @there
    def r3(s):
        arrive(x1r[s].at[0], rs_r.at[s, 6])
        arrive(x1r[s].at[1], rs_r.at[s, 7])

        def x_sum(j):
            return plus(g[s][j, x, c, :low[s]], x1r[s][0, j]) + x1r[s][1, j].astype(F32)

        for k in (3, 2, 1):
            j = zup[k]
            g[s][j, x, c, :low[s]] = x_sum(j).astype(BF16)
            send(g[s].at[j, x, c, lows[s]], zr[s].at[k - 1], rs_s.at[s, 7 + k], rs_r.at[s, 7 + k], dev(j, x, c))
        wg[: low[s], start[s] : start[s] + width[s]] = x_sum(z)
        if MIXED[s]:
            hop(s, 3)

    @if_mixed
    def r4(s):
        @pl.when(z > 0)
        def _():
            arrive(zc[s].at[0, 2], rs_r.at[s, 13])
            g[s][z, :, c, first:] = plus(g[s][z, :, c, first:], zc[s][0, 2]).astype(BF16)

        @pl.when(z < NZ - 1)
        def _():
            arrive(zc[s].at[1, 2], rs_r.at[s, 16])
            g[s][z, :, c, first:] = plus(g[s][z, :, c, first:], zc[s][1, 2]).astype(BF16)

        send(g[s].at[z, xo, c, hi0], hx2[s].at[0], rs_s.at[s, 17], rs_r.at[s, 17], DP)
        send(g[s].at[z, xo, c, hi1], hx2[s].at[1], rs_s.at[s, 18], rs_r.at[s, 18], DM)

    @if_mixed
    def r5(s):
        arrive(hx2[s].at[0], rs_r.at[s, 17])
        g[s][z, xp, c, first : first + half] = plus(g[s][z, xp, c, first : first + half], hx2[s][0]).astype(BF16)
        send(g[s].at[z, xp, c, hi], hx1[s].at[0], rs_s.at[s, 19], rs_r.at[s, 19], DP)
        arrive(hx2[s].at[1], rs_r.at[s, 18])
        g[s][z, xm, c, first + half :] = plus(g[s][z, xm, c, first + half :], hx2[s][1]).astype(BF16)
        send(g[s].at[z, xm, c, hi], hx1[s].at[1], rs_s.at[s, 20], rs_r.at[s, 20], DM)

    @there
    def r6(s):
        here = slice(start[s], start[s] + width[s])
        total = wg[: low[s], here]
        for k in (1, 2, 3):
            arrive(zr[s].at[k - 1], rs_r.at[s, 7 + k])
            total = total + zr[s][k - 1].astype(F32)
        wg[: low[s], here] = total * scale
        if MIXED[s]:
            arrive(hx1[s].at[0], rs_r.at[s, 19])
            arrive(hx1[s].at[1], rs_r.at[s, 20])
            rest = plus(g[s][z, x, c, first:], hx1[s][0]) + hx1[s][1].astype(F32)
            wg[first:, here] = rest * scale
        wg_out(s).start()

    def delta_send():
        code_in.wait()
        scale_in.wait()
        for q in range(NY):
            for b in range(quarter // BLOCK):
                at_col = q * quarter + b * BLOCK
                levels = code[:, at_col : at_col + BLOCK]
                v = jnp.full(levels.shape, table[0], F32)
                for i in range(1, table.shape[0]):
                    v = jnp.where(levels == i, table[i], v)
                n = at_col // BLOCK
                dl[q, :, b * BLOCK : (b + 1) * BLOCK] = v * bscale[:, n : n + 1]
        for k in (1, 2, 3):
            send(dl.at[yup[k]], dyr.at[k - 1], dl_s.at[k - 1], dl_r.at[k - 1], (yup[k] * NH + h, f))

    def delta_pair():
        total = dl[y]
        for k in (1, 2, 3):
            arrive(dyr.at[k - 1], dl_r.at[k - 1])
            total = total + dyr[k - 1]
        dz[0] = total.astype(BF16)
        send(dz.at[0], dz.at[1], dl_s.at[3], dl_r.at[3], DH)

    def delta_share():
        arrive(dz.at[1], dl_r.at[3])
        mean[y] = plus(dz[0], dz[1]) / (NY * NH)
        for k in (1, 2, 3):
            send(mean.at[y], mean.at[y], dl_s.at[3 + k], dl_r.at[3 + k], (yup[k] * NH + h, f))

    def mean_out(q):
        return pltpu.make_async_copy(mean.at[q], mean_hbm.at[:, pl.ds(q * quarter, quarter)], msem.at[q])

    def delta_out():
        for k in (1, 2, 3):
            arrive(mean.at[ydn[k]], dl_r.at[3 + k])
        for q in range(NY):
            mean_out(q).start()

    z_send(0)
    z_send(1)
    h1_send(1)
    delta_send()
    z_wait(0)
    x1_send(0)
    d_send(0, 3)
    h2_send(1)
    z_send(2)
    h1_send(2)
    transpose()
    delta_pair()
    z_wait(1)
    x1_send(1)
    d_send(1, 3)
    for i in range(parts + 1):
        h2_wait(i + 1)
        hop_send(i + 1, 1)
        hop_wait(i, 2)
        hop_send(i, 3)
        x2_send(i)
        d_send(i, 1)
        d_send(i, 2)
        z_send(i + 3)
        h1_send(i + 3)
        h2_send(i + 2)
        z_wait(i + 2)
        x1_send(i + 2)
        d_send(i + 2, 3)
        r1(i - 2)
        r2(i - 3)
        r3(i - 4)
        d_wait(i - 1)
        project(i - 1)
        x2_wait(i)
        d_send(i, 0)
        hop_wait(i + 1, 1)
        hop_send(i + 1, 2)
        for k in range(4):
            grad_rows(i - 1, k)
        hop_wait(i, 3)
        d_send_hi(i)
        if i == 1:
            delta_share()
        if i == 2:
            delta_out()
    for i in range(parts + 1, parts + 5):
        r1(i - 2)
        r2(i - 3)
        r3(i - 4)
        r4(i - 5)
        r5(i - 6)
        r6(i - 6)
        back(i - parts - 1)
    r6(parts - 1)

    for cp, cond in sent:
        if cond is None:
            cp.wait_send()
        else:
            pl.when(cond)(cp.wait_send)
    for j in range(NZ):
        ig_out(j).wait()
    for s in range(parts):
        wg_out(s).wait()
    for q in range(NY):
        mean_out(q).wait()


def inner_step(activations, key_target, key_weight, delta_codes, block_scale, code_table):
    tokens, d = activations.shape
    rows, kv = key_weight.shape
    frag = delta_codes.shape[0]
    widths = [kv * n // sum(WIDTHS) for n in WIDTHS]
    parts = len(widths)
    half = rows // 9
    nhi = 2 * half
    low = [rows - nhi * m for m in MIXED]
    dma = pltpu.SemaphoreType.DMA

    def each(*shape):
        return [pltpu.VMEM(shape + (cw,), BF16) for cw in widths]

    anywhere = pl.BlockSpec(memory_space=pl.ANY)
    return pl.pallas_call(
        kernel,
        out_shape=(
            jax.ShapeDtypeStruct((rows, kv), F32),
            jax.ShapeDtypeStruct((tokens, d), BF16),
            jax.ShapeDtypeStruct((frag, d), F32),
        ),
        in_specs=[pl.BlockSpec(memory_space=pltpu.SMEM)] + [anywhere] * 5,
        out_specs=[anywhere] * 3,
        scratch_shapes=[
            pltpu.VMEM((tokens, d), BF16),
            pltpu.VMEM((NZ, NX, NC * rows, tokens), BF16),
            each(tokens),
            each(NZ, NX, NC, rows),
            each(tokens),
            each(NZ, NX, NC, rows),
            each(NZ, NX, rows),
            [pltpu.VMEM((2, 2, n, cw), BF16) for n, cw in zip(low, widths)],
            [pltpu.VMEM((2, NZ, n, cw), BF16) for n, cw in zip(low, widths)],
            [pltpu.VMEM((NZ - 1, n, cw), BF16) for n, cw in zip(low, widths)],
            each(2, NZ - 1, NX, nhi),
            each(2, half),
            each(2, nhi),
            pltpu.VMEM((rows, kv), F32),
            pltpu.VMEM((tokens, d), BF16),
            pltpu.VMEM(delta_codes.shape, jnp.int32),
            pltpu.VMEM(block_scale.shape, F32),
            pltpu.VMEM((NY, frag, d // NY), F32),
            pltpu.VMEM((NY - 1, frag, d // NY), F32),
            pltpu.VMEM((NH, frag, d // NY), BF16),
            pltpu.VMEM((NY, frag, d // NY), F32),
            dma,
            dma((2,)),
            dma((parts,)),
            dma((parts,)),
            dma((parts,)),
            dma((NZ,)),
            dma((NY,)),
            dma((parts, 22)),
            dma((parts, 22)),
            dma((parts, 21)),
            dma((parts, 21)),
            dma((7,)),
            dma((7,)),
        ],
        compiler_params=pltpu.CompilerParams(
            collective_id=0, has_side_effects=True, vmem_limit_bytes=60 * 2**20
        ),
        cost_estimate=pl.CostEstimate(
            flops=6 * tokens * d * kv, bytes_accessed=64 * 2**20, transcendentals=0
        ),
        name="inner_step",
    )(code_table, activations, key_target, key_weight, delta_codes, block_scale)


def finish_kernel(
    wg_in, ig_in, mean_in, base_in, mom_in, wg_out, ig_out, base_out, mom_out,
    wg, ig, mean, base, mom, base_next, mom_next, sem_in, sem_out,
):
    n = sem_in.shape[0] - 4
    rows = ig.shape[0] // n

    def piece(ref, i):
        return ref.at[pl.ds(i * rows, rows)]

    small = [(mean_in, mean), (base_in, base), (mom_in, mom), (wg_in, wg)]
    get = [pltpu.make_async_copy(u, v, sem_in.at[n + i]) for i, (u, v) in enumerate(small)]
    fetch = [pltpu.make_async_copy(piece(ig_in, i), piece(ig, i), sem_in.at[i]) for i in range(n)]
    done = [pltpu.make_async_copy(piece(ig, i), piece(ig_out, i), sem_out.at[i]) for i in range(n)]
    small = [(base_next, base_out), (mom_next, mom_out), (wg, wg_out)]
    put = [pltpu.make_async_copy(u, v, sem_out.at[n + i]) for i, (u, v) in enumerate(small)]
    for cp in fetch[:2] + get + fetch[2:]:
        cp.start()
    for i in range(2):
        fetch[i].wait()
        done[i].start()
    for cp in get[:3]:
        cp.wait()
    base_next[...], mom_next[...] = outer_update(mean[...], base[...], mom[...])
    put[0].start()
    put[1].start()
    get[3].wait()
    put[2].start()
    for i in range(2, n):
        fetch[i].wait()
        done[i].start()
    for cp in done + put:
        cp.wait()


def finish(weight_grad, input_grad, mean_delta, base, momentum):
    pieces = 8
    anywhere = pl.BlockSpec(memory_space=pl.ANY)

    def like(v):
        return pltpu.VMEM(v.shape, v.dtype)

    outs = (weight_grad, input_grad, base, momentum)
    return pl.pallas_call(
        finish_kernel,
        out_shape=[jax.ShapeDtypeStruct(v.shape, v.dtype) for v in outs],
        in_specs=[anywhere] * 5,
        out_specs=[anywhere] * 4,
        scratch_shapes=[like(v) for v in (weight_grad, input_grad, mean_delta, base, momentum, base, momentum)]
        + [pltpu.SemaphoreType.DMA((pieces + 4,)), pltpu.SemaphoreType.DMA((pieces + 3,))],
        compiler_params=pltpu.CompilerParams(vmem_limit_bytes=60 * 2**20),
        name="finish",
    )(weight_grad, input_grad, mean_delta, base, momentum)


def body(
    activations,
    key_target,
    key_weight,
    fragment_base,
    fragment_momentum,
    delta_codes,
    block_scale,
    code_table,
):
    weight_grad, input_grad, mean_delta = inner_step(
        activations, key_target, key_weight, delta_codes, block_scale, code_table
    )
    weight_grad, input_grad, new_base, new_momentum = finish(
        weight_grad, input_grad, mean_delta, fragment_base, fragment_momentum
    )
    return (weight_grad, input_grad, new_base, new_momentum)


def solution(mesh):
    placed = (
        P(("worker", "fsdp"), None),
        P(("worker", "fsdp"), None),
        P(("worker", "fsdp"), None),
        P("fsdp", None),
        P("fsdp", None),
        P(("worker", "fsdp"), None),
        P(("worker", "fsdp"), None),
        P(),
    )
    return jax.shard_map(
        body,
        mesh=mesh,
        in_specs=placed,
        out_specs=(
            P(("worker", "fsdp"), None),
            P(("worker", "fsdp"), None),
            P("fsdp", None),
            P("fsdp", None),
        ),
        check_vma=False,
    )
```

```python
import jax
import jax.numpy as jnp
from jax import lax
from jax.experimental import pallas as pl
from jax.experimental.pallas import tpu as pltpu
from jax.sharding import PartitionSpec as P

BLOCK = 128
NZ, NX, NC = 4, 4, 2
NY, NH = 4, 2
WIDTHS = (2, 2, 2, 2)
MIXED = (0, 1, 1, 1)
MIXED_BACK = (1, 1, 1, 0)

MESH = pl.DeviceIdType.MESH
F32, BF16 = jnp.float32, jnp.bfloat16

outer_rate = 0.7
outer_momentum = 0.9


def outer_update(mean_delta, base_rows, momentum_rows):
    momentum_next = outer_momentum * momentum_rows + mean_delta
    base_next = base_rows - outer_rate * (mean_delta + outer_momentum * momentum_next)
    return (base_next, momentum_next)


def kernel(
    table, a_hbm, t_hbm, w_hbm, code_hbm, scale_hbm,
    wg_hbm, ig_hbm, mean_hbm,
    a, at, t, w, e, g, dr, x2r, x1r, zr, zc, hx2, hx1, wg, ig,
    code, bscale, dl, dyr, dz, mean,
    lsem, csem, wsem, tsem, osem, isem, msem,
    ag_s, ag_r, rs_s, rs_r, dl_s, dl_r,
    gh_s, gh_r, gp_s, gp_r, rh_s, rh_r, rp_s, rp_r,
):
    parts = len(w)
    mix = [sum(MIXED[:s]) for s in range(parts)]
    mix_r = [sum(MIXED_BACK[:s]) for s in range(parts)]
    tokens, d = a.shape
    rows = w[0].shape[3]
    width = [p.shape[4] for p in w]
    start = [sum(width[:s]) for s in range(parts)]
    half = rows // 9
    low = [rows - 2 * half * m for m in MIXED]
    lows = [pl.ds(0, n) for n in low]
    low_r = [rows - 2 * half * m for m in MIXED_BACK]
    lows_r = [pl.ds(0, n) for n in low_r]
    first = rows - 2 * half
    hi, hi0, hi1 = pl.ds(first, 2 * half), pl.ds(first, half), pl.ds(first + half, half)
    scale = 1.0 / (tokens * NZ * NX * NC) ** 0.5
    slab = d // NZ
    quarter = d // NY

    wk = lax.axis_index("worker")
    f = lax.axis_index("fsdp")
    y, h = wk // NH, lax.rem(wk, NH)
    z, x, c = f // (NX * NC), lax.rem(f // NC, NX), lax.rem(f, NC)
    xp, xm, xo, co = lax.rem(x + 1, NX), lax.rem(x + 3, NX), lax.rem(x + 2, NX), 1 - c
    lines = (xo, xp, xm, x)

    def dev(zz, xx, cc):
        return (wk, (zz * NX + xx) * NC + cc)

    zup = [lax.rem(z + k, NZ) for k in range(NZ)]
    zdn = [lax.rem(z + NZ - k, NZ) for k in range(NZ)]
    yup = [lax.rem(y + k, NY) for k in range(NY)]
    ydn = [lax.rem(y + NY - k, NY) for k in range(NY)]
    DP, DM, DS = dev(z, xp, c), dev(z, xm, c), dev(z, x, co)
    DU, DD = dev(lax.rem(z + 1, NZ), x, c), dev(lax.rem(z + 3, NZ), x, c)
    DH = (y * NH + 1 - h, f)

    def cols(s):
        return pl.ds(start[s], width[s])

    def w_in(s):
        return pltpu.make_async_copy(w_hbm.at[:, cols(s)], w[s].at[z, x, c], wsem.at[s])

    def t_in(s):
        return pltpu.make_async_copy(t_hbm.at[:, cols(s)], t[s], tsem.at[s])

    a_in = pltpu.make_async_copy(a_hbm, a, lsem)
    code_in = pltpu.make_async_copy(code_hbm, code, csem.at[0])
    scale_in = pltpu.make_async_copy(scale_hbm, bscale, csem.at[1])

    for s in range(parts):
        w_in(s).start()
    code_in.start()
    scale_in.start()
    a_in.start()
    for s in range(parts):
        t_in(s).start()

    barrier = pltpu.get_barrier_semaphore()
    partners = [dev(zup[k], x, c) for k in (1, 2, 3)] + [DP, DM, DS, DH]
    partners += [(yup[k] * NH + h, f) for k in (1, 2, 3)]
    for p in partners:
        pl.semaphore_signal(barrier, inc=1, device_id=p, device_id_type=MESH)
    pl.semaphore_wait(barrier, len(partners))

    sent = []

    def send(src, dst, ss, rs, to, cond=None, group=False):
        cp = pltpu.make_async_remote_copy(
            src_ref=src, dst_ref=dst, send_sem=ss, recv_sem=rs, device_id=to, device_id_type=MESH
        )
        if cond is None:
            cp.start()
        else:
            pl.when(cond)(cp.start)
        if not group:
            sent.append((cp, cond))

    def arrive(dst, rs):
        pltpu.make_async_remote_copy(
            src_ref=dst, dst_ref=dst, send_sem=rs, recv_sem=rs, device_id=DS, device_id_type=MESH
        ).wait_recv()

    def guard(ok):
        def wrap(step):
            def run(s, *k):
                if ok(s):
                    step(s, *k)

            return run

        return wrap

    there = guard(lambda s: 0 <= s < parts)
    if_mixed = guard(lambda s: 0 <= s < parts and MIXED[s])
    if_mixed_r = guard(lambda s: 0 <= s < parts and MIXED_BACK[s])

    @there
    def z_send(s):
        for k in (3, 2, 1):
            blk = w[s].at[z, x, c, lows[s]]
            send(blk, blk, ag_s.at[s, 0], ag_r.at[s, k - 1], dev(zup[k], x, c), group=True)

    @there
    def z_wait(s):
        for k in (1, 2, 3):
            arrive(w[s].at[zdn[k], x, c, lows[s]], ag_r.at[s, k - 1])

    @there
    def x1_send(s):
        line = w[s].at[:, x, c, lows[s]]
        send(line, line, ag_s.at[s, 1], ag_r.at[s, 3], DP, group=True)
        send(line, line, ag_s.at[s, 1], ag_r.at[s, 4], DM, group=True)

    @there
    def x2_send(s):
        arrive(w[s].at[:, xm, c, lows[s]], ag_r.at[s, 3])
        up = w[s].at[pl.ds(0, 2), xm, c, lows[s]]
        send(up, up, ag_s.at[s, 2], ag_r.at[s, 5], DP, group=True)
        arrive(w[s].at[:, xp, c, lows[s]], ag_r.at[s, 4])
        down = w[s].at[pl.ds(2, 2), xp, c, lows[s]]
        send(down, down, ag_s.at[s, 2], ag_r.at[s, 6], DM, group=True)

    @there
    def x2_wait(s):
        arrive(w[s].at[pl.ds(0, 2), xo, c, lows[s]], ag_r.at[s, 5])
        arrive(w[s].at[pl.ds(2, 2), xo, c, lows[s]], ag_r.at[s, 6])

    @there
    def d_send(s, k):
        line = w[s].at[:, lines[k], c, lows[s]]
        send(line, line, ag_s.at[s, 3], ag_r.at[s, 7 + k], DS, group=True)

    @if_mixed
    def d_send_hi(s):
        rest = w[s].at[:, :, c, hi]
        send(rest, rest, gh_s.at[mix[s], 0], gh_r.at[mix[s], 0], DS)

    @there
    def d_wait(s):
        for k in range(4):
            arrive(w[s].at[:, lines[k], co, lows[s]], ag_r.at[s, 7 + k])
        if MIXED[s]:
            arrive(w[s].at[:, :, co, hi], gh_r.at[mix[s], 0])

    @if_mixed
    def h1_send(s):
        blk = w[s].at[z, x, c, hi]
        send(blk, blk, gh_s.at[mix[s], 1], gh_r.at[mix[s], 1], DP, group=True)
        send(blk, blk, gh_s.at[mix[s], 1], gh_r.at[mix[s], 2], DM, group=True)

    @if_mixed
    def h2_send(s):
        arrive(w[s].at[z, xm, c, hi], gh_r.at[mix[s], 1])
        up = w[s].at[z, xm, c, hi0]
        send(up, up, gh_s.at[mix[s], 2], gh_r.at[mix[s], 3], DP, group=True)
        arrive(w[s].at[z, xp, c, hi], gh_r.at[mix[s], 2])
        down = w[s].at[z, xp, c, hi1]
        send(down, down, gh_s.at[mix[s], 2], gh_r.at[mix[s], 4], DM, group=True)

    @if_mixed
    def h2_wait(s):
        arrive(w[s].at[z, xo, c, hi0], gh_r.at[mix[s], 3])
        arrive(w[s].at[z, xo, c, hi1], gh_r.at[mix[s], 4])

    @if_mixed
    def hop_send(s, k):
        up, dn = w[s].at[zdn[k - 1], :, c, hi], w[s].at[zup[k - 1], :, c, hi]
        send(up, up, gp_s.at[mix[s], k - 1], gp_r.at[mix[s], k - 1], DU, (z >= k - 1) & (z < NZ - 1))
        send(dn, dn, gp_s.at[mix[s], k + 2], gp_r.at[mix[s], k + 2], DD, (z + k <= NZ) & (z > 0))

    @if_mixed
    def hop_wait(s, k):
        pl.when(z >= k)(lambda: arrive(w[s].at[zdn[k], :, c, hi], gp_r.at[mix[s], k - 1]))
        pl.when(z + k < NZ)(lambda: arrive(w[s].at[zup[k], :, c, hi], gp_r.at[mix[s], k + 2]))

    def transpose():
        a_in.wait()
        for j in range(NZ):
            at[j] = a[:, j * slab : (j + 1) * slab].T.reshape(NX, NC * rows, tokens)

    @there
    def project(s):
        t_in(s).wait()
        p = jnp.dot(a[...], w[s][...].reshape(d, width[s]), preferred_element_type=F32)
        e[s][...] = (p - t[s][...].astype(F32)).astype(BF16)

    @there
    def grad_rows(s, k):
        xt = lines[k]
        q = jnp.dot(at[:, xt].reshape(slab, tokens), e[s][...], preferred_element_type=F32)
        g[s][:, xt] = q.astype(BF16).reshape(NZ, NC, rows, width[s])
        send(g[s].at[:, xt, co], dr[s].at[:, xt], rs_s.at[s, 0], rs_r.at[s, k], DS, group=True)

    def back(j):
        er = jnp.concatenate([e[s][...] for s in range(parts)], axis=1)
        wr = jnp.concatenate([w[s][j].reshape(slab, width[s]) for s in range(parts)], axis=1)
        q = lax.dot_general(er, wr, (((1,), (1,)), ((), ())), preferred_element_type=F32)
        ig[:, j * slab : (j + 1) * slab] = q.astype(BF16)
        ig_out(j).start()

    def ig_out(j):
        here = pl.ds(j * slab, slab)
        return pltpu.make_async_copy(ig.at[:, here], ig_hbm.at[:, here], isem.at[j])

    def wg_out(s):
        return pltpu.make_async_copy(wg.at[:, cols(s)], wg_hbm.at[:, cols(s)], osem.at[s])

    def plus(u, v):
        return u.astype(F32) + v.astype(F32)

    def merge(s, k):
        xt = lines[k]
        arrive(dr[s].at[:, xt], rs_r.at[s, k])
        g[s][:, xt, c] = plus(g[s][:, xt, c], dr[s][:, xt]).astype(BF16)

    @there
    def r1(s):
        merge(s, 0)
        send(g[s].at[pl.ds(0, 2), xo, c, lows_r[s]], x2r[s].at[0], rs_s.at[s, 1], rs_r.at[s, 4], DP, group=True)
        send(g[s].at[pl.ds(2, 2), xo, c, lows_r[s]], x2r[s].at[1], rs_s.at[s, 1], rs_r.at[s, 5], DM, group=True)
        for k in (1, 2, 3):
            merge(s, k)
        if MIXED_BACK[s]:
            hop(s, 1)

    def hop(s, k):
        up, dn = zup[NZ - k], zdn[NZ - k]
        goes_up, goes_dn = z <= k - 1, z >= NZ - k
        if k > 1:

            @pl.when(goes_up & (z > 0))
            def _():
                arrive(zc[s].at[0, k - 2], rp_r.at[mix_r[s], k - 2])
                g[s][up, :, c, first:] = plus(g[s][up, :, c, first:], zc[s][0, k - 2]).astype(BF16)

            @pl.when(goes_dn & (z < NZ - 1))
            def _():
                arrive(zc[s].at[1, k - 2], rp_r.at[mix_r[s], k + 1])
                g[s][dn, :, c, first:] = plus(g[s][dn, :, c, first:], zc[s][1, k - 2]).astype(BF16)

        send(g[s].at[up, :, c, hi], zc[s].at[0, k - 1], rp_s.at[mix_r[s], k - 1], rp_r.at[mix_r[s], k - 1], DU, goes_up)
        send(g[s].at[dn, :, c, hi], zc[s].at[1, k - 1], rp_s.at[mix_r[s], k + 2], rp_r.at[mix_r[s], k + 2], DD, goes_dn)

    @there
    def r2(s):
        arrive(x2r[s].at[0], rs_r.at[s, 4])
        g[s][0:2, xp, c, :low_r[s]] = plus(g[s][0:2, xp, c, :low_r[s]], x2r[s][0]).astype(BF16)
        send(g[s].at[:, xp, c, lows_r[s]], x1r[s].at[0], rs_s.at[s, 2], rs_r.at[s, 6], DP, group=True)
        arrive(x2r[s].at[1], rs_r.at[s, 5])
        g[s][2:4, xm, c, :low_r[s]] = plus(g[s][2:4, xm, c, :low_r[s]], x2r[s][1]).astype(BF16)
        send(g[s].at[:, xm, c, lows_r[s]], x1r[s].at[1], rs_s.at[s, 2], rs_r.at[s, 7], DM, group=True)
        if MIXED_BACK[s]:
            hop(s, 2)

    @there
    def r3(s):
        arrive(x1r[s].at[0], rs_r.at[s, 6])
        arrive(x1r[s].at[1], rs_r.at[s, 7])

        def x_sum(j):
            return plus(g[s][j, x, c, :low_r[s]], x1r[s][0, j]) + x1r[s][1, j].astype(F32)

        for k in (3, 2, 1):
            j = zup[k]
            g[s][j, x, c, :low_r[s]] = x_sum(j).astype(BF16)
            send(g[s].at[j, x, c, lows_r[s]], zr[s].at[k - 1], rs_s.at[s, 3], rs_r.at[s, 7 + k], dev(j, x, c), group=True)
        wg[: low_r[s], start[s] : start[s] + width[s]] = x_sum(z)
        if MIXED_BACK[s]:
            hop(s, 3)

    @if_mixed_r
    def r4(s):
        @pl.when(z > 0)
        def _():
            arrive(zc[s].at[0, 2], rp_r.at[mix_r[s], 2])
            g[s][z, :, c, first:] = plus(g[s][z, :, c, first:], zc[s][0, 2]).astype(BF16)

        @pl.when(z < NZ - 1)
        def _():
            arrive(zc[s].at[1, 2], rp_r.at[mix_r[s], 5])
            g[s][z, :, c, first:] = plus(g[s][z, :, c, first:], zc[s][1, 2]).astype(BF16)

        send(g[s].at[z, xo, c, hi0], hx2[s].at[0], rh_s.at[mix_r[s], 0], rh_r.at[mix_r[s], 0], DP, group=True)
        send(g[s].at[z, xo, c, hi1], hx2[s].at[1], rh_s.at[mix_r[s], 0], rh_r.at[mix_r[s], 1], DM, group=True)

    @if_mixed_r
    def r5(s):
        arrive(hx2[s].at[0], rh_r.at[mix_r[s], 0])
        g[s][z, xp, c, first : first + half] = plus(g[s][z, xp, c, first : first + half], hx2[s][0]).astype(BF16)
        send(g[s].at[z, xp, c, hi], hx1[s].at[0], rh_s.at[mix_r[s], 1], rh_r.at[mix_r[s], 2], DP, group=True)
        arrive(hx2[s].at[1], rh_r.at[mix_r[s], 1])
        g[s][z, xm, c, first + half :] = plus(g[s][z, xm, c, first + half :], hx2[s][1]).astype(BF16)
        send(g[s].at[z, xm, c, hi], hx1[s].at[1], rh_s.at[mix_r[s], 1], rh_r.at[mix_r[s], 3], DM, group=True)

    @there
    def r6(s):
        here = slice(start[s], start[s] + width[s])
        total = wg[: low_r[s], here]
        for k in (1, 2, 3):
            arrive(zr[s].at[k - 1], rs_r.at[s, 7 + k])
            total = total + zr[s][k - 1].astype(F32)
        wg[: low_r[s], here] = total * scale
        if MIXED_BACK[s]:
            arrive(hx1[s].at[0], rh_r.at[mix_r[s], 2])
            arrive(hx1[s].at[1], rh_r.at[mix_r[s], 3])
            rest = plus(g[s][z, x, c, first:], hx1[s][0]) + hx1[s][1].astype(F32)
            wg[first:, here] = rest * scale
        wg_out(s).start()

    def delta_send():
        code_in.wait()
        scale_in.wait()
        for q in range(NY):
            for b in range(quarter // BLOCK):
                at_col = q * quarter + b * BLOCK
                levels = code[:, at_col : at_col + BLOCK]
                v = jnp.full(levels.shape, table[0], F32)
                for i in range(1, table.shape[0]):
                    v = jnp.where(levels == i, table[i], v)
                n = at_col // BLOCK
                dl[q, :, b * BLOCK : (b + 1) * BLOCK] = v * bscale[:, n : n + 1]
        for k in (1, 2, 3):
            send(dl.at[yup[k]], dyr.at[k - 1], dl_s.at[k - 1], dl_r.at[k - 1], (yup[k] * NH + h, f))

    def delta_pair():
        total = dl[y]
        for k in (1, 2, 3):
            arrive(dyr.at[k - 1], dl_r.at[k - 1])
            total = total + dyr[k - 1]
        dz[0] = total.astype(BF16)
        send(dz.at[0], dz.at[1], dl_s.at[3], dl_r.at[3], DH)

    def delta_share():
        arrive(dz.at[1], dl_r.at[3])
        mean[y] = plus(dz[0], dz[1]) / (NY * NH)
        for k in (1, 2, 3):
            send(mean.at[y], mean.at[y], dl_s.at[3 + k], dl_r.at[3 + k], (yup[k] * NH + h, f))

    def mean_out(q):
        return pltpu.make_async_copy(mean.at[q], mean_hbm.at[:, pl.ds(q * quarter, quarter)], msem.at[q])

    def delta_out():
        for k in (1, 2, 3):
            arrive(mean.at[ydn[k]], dl_r.at[3 + k])
        for q in range(NY):
            mean_out(q).start()

    w_in(0).wait()
    z_send(0)
    for s in range(parts):
        if s > 0:
            w_in(s).wait()
        h1_send(s)
    z_send(1)
    delta_send()
    z_wait(0)
    x1_send(0)
    d_send(0, 3)
    for s in range(parts):
        h2_send(s)
    z_send(2)
    transpose()
    z_wait(1)
    x1_send(1)
    d_send(1, 3)
    for s in range(parts):
        h2_wait(s)
        hop_send(s, 1)
    delta_pair()
    for i in range(parts + 1):
        x2_send(i)
        d_send(i, 1)
        d_send(i, 2)
        z_send(i + 3)
        z_wait(i + 2)
        x1_send(i + 2)
        d_send(i + 2, 3)
        r3(i - 4)
        r2(i - 3)
        r1(i - 2)
        d_wait(i - 1)
        project(i - 1)
        if i < 2:
            for s in range(parts):
                hop_wait(s, 1 + i)
                hop_send(s, 2 + i)
        x2_wait(i)
        d_send(i, 0)
        for k in range(4):
            grad_rows(i - 1, k)
        if i == 1:
            for s in range(parts):
                hop_wait(s, 3)
                d_send_hi(s)
            delta_share()
        if i == 2:
            delta_out()
    for i in range(parts + 1, parts + 5):
        r1(i - 2)
        r2(i - 3)
        r3(i - 4)
        r4(i - 5)
        r5(i - 6)
        r6(i - 6)
        back(i - parts - 1)
    r6(parts - 1)

    def all_sent(total, sem):
        pltpu.make_async_remote_copy(
            src_ref=total, dst_ref=total, send_sem=sem, recv_sem=sem, device_id=DS, device_id_type=MESH
        ).wait_send()

    for s in range(parts):
        lo = lows[s]
        all_sent(w[s].at[pl.ds(0, 3), x, c, lo], ag_s.at[s, 0])
        all_sent(w[s].at[:, pl.ds(0, 2), c, lo], ag_s.at[s, 1])
        all_sent(w[s].at[:, x, c, lo], ag_s.at[s, 2])
        all_sent(w[s].at[:, :, c, lo], ag_s.at[s, 3])
        for n, total in enumerate((dr, x2r, x1r, zr)):
            all_sent(total[s], rs_s.at[s, n])
        if MIXED[s]:
            all_sent(w[s].at[z, pl.ds(0, 2), c, hi], gh_s.at[mix[s], 1])
            all_sent(w[s].at[z, x, c, hi], gh_s.at[mix[s], 2])
        if MIXED_BACK[s]:
            all_sent(hx2[s], rh_s.at[mix_r[s], 0])
            all_sent(hx1[s], rh_s.at[mix_r[s], 1])
    for cp, cond in sent:
        if cond is None:
            cp.wait_send()
        else:
            pl.when(cond)(cp.wait_send)
    for j in range(NZ):
        ig_out(j).wait()
    for s in range(parts):
        wg_out(s).wait()
    for q in range(NY):
        mean_out(q).wait()


def inner_step(activations, key_target, key_weight, delta_codes, block_scale, code_table):
    tokens, d = activations.shape
    rows, kv = key_weight.shape
    frag = delta_codes.shape[0]
    widths = [kv * n // sum(WIDTHS) for n in WIDTHS]
    parts = len(widths)
    mixed, mixed_r = max(1, sum(MIXED)), max(1, sum(MIXED_BACK))
    half = rows // 9
    nhi = 2 * half
    low = [rows - nhi * m for m in MIXED_BACK]
    dma = pltpu.SemaphoreType.DMA

    def each(*shape):
        return [pltpu.VMEM(shape + (cw,), BF16) for cw in widths]

    anywhere = pl.BlockSpec(memory_space=pl.ANY)
    return pl.pallas_call(
        kernel,
        out_shape=(
            jax.ShapeDtypeStruct((rows, kv), F32),
            jax.ShapeDtypeStruct((tokens, d), BF16),
            jax.ShapeDtypeStruct((frag, d), F32),
        ),
        in_specs=[pl.BlockSpec(memory_space=pltpu.SMEM)] + [anywhere] * 5,
        out_specs=[anywhere] * 3,
        scratch_shapes=[
            pltpu.VMEM((tokens, d), BF16),
            pltpu.VMEM((NZ, NX, NC * rows, tokens), BF16),
            each(tokens),
            each(NZ, NX, NC, rows),
            each(tokens),
            each(NZ, NX, NC, rows),
            each(NZ, NX, rows),
            [pltpu.VMEM((2, 2, n, cw), BF16) for n, cw in zip(low, widths)],
            [pltpu.VMEM((2, NZ, n, cw), BF16) for n, cw in zip(low, widths)],
            [pltpu.VMEM((NZ - 1, n, cw), BF16) for n, cw in zip(low, widths)],
            each(2, NZ - 1, NX, nhi),
            each(2, half),
            each(2, nhi),
            pltpu.VMEM((rows, kv), F32),
            pltpu.VMEM((tokens, d), BF16),
            pltpu.VMEM(delta_codes.shape, jnp.int32),
            pltpu.VMEM(block_scale.shape, F32),
            pltpu.VMEM((NY, frag, d // NY), F32),
            pltpu.VMEM((NY - 1, frag, d // NY), F32),
            pltpu.VMEM((NH, frag, d // NY), BF16),
            pltpu.VMEM((NY, frag, d // NY), F32),
            dma,
            dma((2,)),
            dma((parts,)),
            dma((parts,)),
            dma((parts,)),
            dma((NZ,)),
            dma((NY,)),
            dma((parts, 4)),
            dma((parts, 11)),
            dma((parts, 4)),
            dma((parts, 11)),
            dma((7,)),
            dma((7,)),
            dma((mixed, 3)),
            dma((mixed, 5)),
            dma((mixed, 6)),
            dma((mixed, 6)),
            dma((mixed_r, 2)),
            dma((mixed_r, 4)),
            dma((mixed_r, 6)),
            dma((mixed_r, 6)),
        ],
        compiler_params=pltpu.CompilerParams(
            collective_id=0, has_side_effects=True, vmem_limit_bytes=60 * 2**20
        ),
        cost_estimate=pl.CostEstimate(
            flops=6 * tokens * d * kv, bytes_accessed=64 * 2**20, transcendentals=0
        ),
        name="inner_step",
    )(code_table, activations, key_target, key_weight, delta_codes, block_scale)


def finish_kernel(
    wg_in, ig_in, mean_in, base_in, mom_in, wg_out, ig_out, base_out, mom_out,
    wg, ig, mean, base, mom, base_next, mom_next, sem_in, sem_out,
):
    n = sem_in.shape[0] - 4
    rows = ig.shape[0] // n

    def piece(ref, i):
        return ref.at[pl.ds(i * rows, rows)]

    small = [(mean_in, mean), (base_in, base), (mom_in, mom), (wg_in, wg)]
    get = [pltpu.make_async_copy(u, v, sem_in.at[n + i]) for i, (u, v) in enumerate(small)]
    fetch = [pltpu.make_async_copy(piece(ig_in, i), piece(ig, i), sem_in.at[i]) for i in range(n)]
    done = [pltpu.make_async_copy(piece(ig, i), piece(ig_out, i), sem_out.at[i]) for i in range(n)]
    small = [(base_next, base_out), (mom_next, mom_out), (wg, wg_out)]
    put = [pltpu.make_async_copy(u, v, sem_out.at[n + i]) for i, (u, v) in enumerate(small)]
    for cp in fetch[:2] + get + fetch[2:]:
        cp.start()
    for i in range(2):
        fetch[i].wait()
        done[i].start()
    for cp in get[:3]:
        cp.wait()
    base_next[...], mom_next[...] = outer_update(mean[...], base[...], mom[...])
    put[0].start()
    put[1].start()
    get[3].wait()
    put[2].start()
    for i in range(2, n):
        fetch[i].wait()
        done[i].start()
    for cp in done + put:
        cp.wait()


def finish(weight_grad, input_grad, mean_delta, base, momentum):
    pieces = 8
    anywhere = pl.BlockSpec(memory_space=pl.ANY)

    def like(v):
        return pltpu.VMEM(v.shape, v.dtype)

    outs = (weight_grad, input_grad, base, momentum)
    return pl.pallas_call(
        finish_kernel,
        out_shape=[jax.ShapeDtypeStruct(v.shape, v.dtype) for v in outs],
        in_specs=[anywhere] * 5,
        out_specs=[anywhere] * 4,
        scratch_shapes=[like(v) for v in (weight_grad, input_grad, mean_delta, base, momentum, base, momentum)]
        + [pltpu.SemaphoreType.DMA((pieces + 4,)), pltpu.SemaphoreType.DMA((pieces + 3,))],
        compiler_params=pltpu.CompilerParams(vmem_limit_bytes=60 * 2**20),
        name="finish",
    )(weight_grad, input_grad, mean_delta, base, momentum)


def body(
    activations,
    key_target,
    key_weight,
    fragment_base,
    fragment_momentum,
    delta_codes,
    block_scale,
    code_table,
):
    weight_grad, input_grad, mean_delta = inner_step(
        activations, key_target, key_weight, delta_codes, block_scale, code_table
    )
    weight_grad, input_grad, new_base, new_momentum = finish(
        weight_grad, input_grad, mean_delta, fragment_base, fragment_momentum
    )
    return (weight_grad, input_grad, new_base, new_momentum)


def solution(mesh):
    placed = (
        P(("worker", "fsdp"), None),
        P(("worker", "fsdp"), None),
        P(("worker", "fsdp"), None),
        P("fsdp", None),
        P("fsdp", None),
        P(("worker", "fsdp"), None),
        P(("worker", "fsdp"), None),
        P(),
    )
    return jax.shard_map(
        body,
        mesh=mesh,
        in_specs=placed,
        out_specs=(
            P(("worker", "fsdp"), None),
            P(("worker", "fsdp"), None),
            P("fsdp", None),
            P("fsdp", None),
        ),
        check_vma=False,
    )
```
